128 devices in a mesh: pair: 32 (over z, y, core), aux: 4 (over x).
Axes of the slice: x: 4, y: 4, z: 4, core: 2. Of those that a mesh axis runs over, the one named last changes fastest.
Arguments:
- ac_factors: bfloat16 [9600, 128], P('aux'), may hold values from -6 to 6
- bd_factors: bfloat16 [2400, 4, 38400], P('pair', 'aux'), may hold values from -0.0625 to 0.0625
- amplitudes: float32 [24576, 8, 2400], P(('pair', 'aux')), may hold values from -0.046875 to 0.046875
Outputs:
- ladder: float32 [24576, 256], P(('pair', 'aux'))
The draws below stay inside these ranges and needn't reach their ends.
All inputs are finite; a program needn't handle non-finite values.
Results may differ from the reference program's by a relative error of at most 0.0003.
Values sent between devices are 32-bit elements; how exact they have to be, the bound alone decides.
No kernel may reach another device: no remote copies, remote signals or barrier semaphores. Data moves between devices by JAX's collectives and lax.ppermute only.
A program may use at most 192 MiB of HBM per device.

```python
import jax
import jax.numpy as jnp
from jax import lax

V = 2400
NAUX = 9600
NA = 16
NC = 8
NB = 16
PAIRS = 24576
N_AUX = 4


def steps_of(own_key, shape, cuts, smallest, largest):
    def one(position, blocks):
        draws = jax.random.uniform(jax.random.fold_in(jax.random.fold_in(own_key, 6), position), (blocks,), jnp.float32, smallest / len(cuts), largest / len(cuts))
        return jnp.repeat(jnp.exp(draws), shape[position] // blocks).reshape((-1,) + (1,) * (len(shape) - position - 1))

    gain = one(*cuts[0])
    for cut in cuts[1:]:
        gain = gain * one(*cut)
    return gain


def scatter_about(own_key, dims, scale, reach, pieces=(), dtype=jnp.bfloat16):
    loudness = steps_of(own_key, dims, pieces, -0.22, 0.18) if pieces else 1.0
    entries = jax.random.normal(own_key, dims, jnp.float32) * scale * loudness
    return jnp.minimum(jnp.maximum(entries, -reach), reach).astype(dtype)


def setup_inputs(seed: int = 0) -> dict:
    keys = jax.random.split(jax.random.key(seed), 4)
    ac_factors = scatter_about(keys[0], (NAUX, NA * NC), 1.0, 6.0, ((0, 4),))
    bd_factors = scatter_about(keys[1], (V, N_AUX, NB * (NAUX // N_AUX)), NAUX ** -0.5, 0.0625, ((0, 32), (1, 4)))
    amplitudes = scatter_about(keys[2], (PAIRS, NC, V), (NC * V) ** -0.5, 0.046875, ((0, 128),), jnp.float32)
    return dict(ac_factors=ac_factors, bd_factors=bd_factors, amplitudes=amplitudes)


def reference(ac_factors, bd_factors, amplitudes):
    slice_rows = NAUX // N_AUX
    summed = jnp.zeros((V * NB, NA * NC), jnp.float32)
    for k in range(N_AUX):
        block = bd_factors[:, k, :].reshape(V * NB, slice_rows)
        factor_rows = ac_factors[k * slice_rows:(k + 1) * slice_rows, :]
        summed = summed + jnp.dot(block, factor_rows, preferred_element_type=jnp.float32)
    integrals = summed.reshape(V, NB, NA * NC).transpose(2, 1, 0).reshape(NA, NC, NB, V)
    result = jnp.einsum("pcd,acbd->pab", amplitudes, integrals, precision=lax.Precision.HIGHEST)
    return result.reshape(PAIRS, NA * NB)
```

```python
import functools

import jax
import jax.numpy as jnp
from jax import lax
from jax.experimental import pallas as pl
from jax.experimental.pallas import tpu as pltpu
from jax.sharding import PartitionSpec as P

AXES = ("pair", "aux")
SIDE = 4
CORES = 2
CHIP_ROWS = 150
FRAME = 152
PARTS = ((0, 48, "xyz"), (48, 96, "yzx"), (96, 152, "zxy"))
WIDE = 16 * 56
REL = (0, 1, 3, 2)


def place(z, y, core, x):
    return (((z % SIDE) * SIDE + y % SIDE) * CORES + core) * SIDE + x % SIDE


def permute(value, step, axis, signed=True):
    pairs = []
    for z in range(SIDE):
        for y in range(SIDE):
            for core in range(CORES):
                for x in range(SIDE):
                    s = -step if signed and core else step
                    to = dict(z=z, y=y, core=core, x=x)
                    if axis == "core":
                        to["core"] = 1 - core
                    else:
                        to[axis] += s
                    pairs.append((place(z, y, core, x), place(**to)))
    return lax.ppermute(value, AXES, pairs)


def partial_kernel(slot_ref, bd_ref, ac_ref, swap_ref, out_ref, shifted):
    rows = ac_ref.shape[0]
    count_d = bd_ref.shape[0]
    block_b = bd_ref.shape[1] // rows
    ordered = jnp.dot(ac_ref[...], swap_ref[...], preferred_element_type=jnp.float32).astype(jnp.bfloat16)
    shifted[...] = jnp.zeros_like(shifted)
    for k in range(4):
        shifted[k, pl.ds((rows * k) % 128, rows), :] = ordered
    products = []
    for b in range(block_b):
        offset = (rows * b) % 128
        start = rows * b - offset
        length = -(-(offset + rows) // 128) * 128
        products.append(jnp.dot(bd_ref[:, start:start + length], shifted[b % 4, :length, :],
                                preferred_element_type=jnp.float32))
    out_ref[...] = jnp.zeros_like(out_ref)
    core = slot_ref[8]
    slabs = [jnp.concatenate([p[:, 16 * c:16 * c + 16] for p in products], axis=1) for c in range(8)]
    for which in range(CORES):
        @pl.when(core == which)
        def _():
            for c in range(8):
                out_ref[slot_ref[c], which * count_d:(which + 1) * count_d, :] = slabs[c]


def partial_integrals(slots, bd, ac, swap):
    rows = ac.shape[0]
    return pl.pallas_call(
        partial_kernel,
        out_shape=jax.ShapeDtypeStruct((8, FRAME, 256), jnp.float32),
        in_specs=[pl.BlockSpec(memory_space=pltpu.SMEM)] + [pl.BlockSpec(memory_space=pltpu.VMEM)] * 3,
        out_specs=pl.BlockSpec(memory_space=pltpu.VMEM),
        scratch_shapes=[pltpu.VMEM((4, -(-(rows + 96) // 128) * 128, 128), jnp.bfloat16)],
        compiler_params=pltpu.CompilerParams(vmem_limit_bytes=40 * 2**20),
        cost_estimate=pl.CostEstimate(flops=10**9, bytes_accessed=8 * 10**6, transcendentals=0),
    )(slots, bd, ac, swap)


def arrange_kernel(amp_ref, out_ref):
    for c in range(8):
        half, x = divmod(c, SIDE)
        row = amp_ref[:, c, :]
        row = jnp.concatenate([row, jnp.zeros((row.shape[0], 32), jnp.float32)], axis=1)
        for z in range(SIDE):
            for y in range(SIDE):
                at = dict(x=x, y=y, z=z)
                for j, (first, last, order) in enumerate(PARTS):
                    inner = (at[order[1]] * SIDE + at[order[0]]) * (last - first)
                    begin = CHIP_ROWS * (z * SIDE + y) + first
                    out_ref[half, SIDE * j + at[order[2]], :, inner:inner + last - first] = row[:, begin:begin + last - first]


def arrange(amps):
    pairs = amps.shape[0]
    step = 16
    return pl.pallas_call(
        arrange_kernel,
        grid=(pairs // step,),
        out_shape=jax.ShapeDtypeStruct((2, 12, pairs, WIDE), jnp.float32),
        in_specs=[pl.BlockSpec((step,) + amps.shape[1:], lambda i: (i, 0, 0))],
        out_specs=pl.BlockSpec((2, 12, step, WIDE), lambda i: (0, 0, i, 0)),
        compiler_params=pltpu.CompilerParams(vmem_limit_bytes=40 * 2**20),
        cost_estimate=pl.CostEstimate(flops=10**6, bytes_accessed=30 * 10**6, transcendentals=0),
    )(amps)


def split(value):
    high = value.astype(jnp.bfloat16)
    return high, (value - high.astype(jnp.float32)).astype(jnp.bfloat16)


def ladder_kernel(piece_ref, own_ref, other_ref, order_ref, *refs):
    pieces, out_ref, total = refs[:15], refs[15], refs[16]
    step = pl.program_id(0)

    @pl.when(step == 0)
    def _():
        total[...] = jnp.zeros_like(total)

    for k in range(12):
        @pl.when(step == k)
        def _():
            j, kind = divmod(k, 4)
            if kind < 3:
                block = pieces[5 * j + kind][...]
            else:
                block = jnp.concatenate([pieces[5 * j + 3][...], pieces[5 * j + 4][...]], axis=0)
            high, low = split(block)
            depth = block.shape[0]
            for r, amp_ref in enumerate((own_ref, other_ref)):
                ahigh, alow = split(amp_ref[:, :depth])
                dot = functools.partial(jnp.dot, preferred_element_type=jnp.float32)
                total[r] += dot(ahigh, high) + (dot(ahigh, low) + dot(alow, high))

    @pl.when(step == 11)
    def _():
        for r in range(2):
            out_ref[r] = jnp.dot(total[r], order_ref[...], precision=lax.Precision.HIGHEST,
                                 preferred_element_type=jnp.float32)


def ladder(ids, own, other, order, pieces):
    pairs = own.shape[1]
    amp_spec = pl.BlockSpec((None, pairs, WIDE), lambda k, ids: (ids[k], 0, 0))
    whole = pl.BlockSpec(memory_space=pltpu.VMEM)
    return pl.pallas_call(
        ladder_kernel,
        grid_spec=pltpu.PrefetchScalarGridSpec(
            num_scalar_prefetch=1,
            grid=(12,),
            in_specs=[amp_spec, amp_spec, whole] + [whole] * 15,
            out_specs=whole,
            scratch_shapes=[pltpu.VMEM((2, pairs, 256), jnp.float32)],
        ),
        out_shape=jax.ShapeDtypeStruct((2, pairs, 256), jnp.float32),
        compiler_params=pltpu.CompilerParams(vmem_limit_bytes=40 * 2**20),
        cost_estimate=pl.CostEstimate(flops=6 * 10**9, bytes_accessed=25 * 10**6, transcendentals=0),
    )(ids, own, other, order, *pieces)


def gather(value, axis, coord, sign):
    rows = value.shape[0]
    got = ((coord, value), (coord - sign, permute(value, 1, axis)), (coord + sign, permute(value, -1, axis)),
           (coord + 2, permute(value, 2, axis)))
    whole = jnp.zeros((SIDE * rows, value.shape[1]), jnp.float32)
    for at, block in got:
        whole = lax.dynamic_update_slice(whole, block, ((at % SIDE) * rows, 0))
    return whole


def body(ac_factors, bd_factors, amplitudes):
    pair, x = lax.axis_index("pair"), lax.axis_index("aux")
    core = pair % CORES
    at = dict(x=x, y=(pair // CORES) % SIDE, z=pair // (CORES * SIDE))
    sign = 1 - 2 * core
    column = jnp.arange(128)
    swap = (column[:, None] % 8 * 16 + column[:, None] // 8 == column[None, :]).astype(jnp.bfloat16)
    column = jnp.arange(256)
    order = (column[:, None] % 16 * 16 + column[:, None] // 16 == column[None, :]).astype(jnp.float32)
    c = jnp.arange(8)
    ahead = (c % SIDE - x) % SIDE
    slot = jnp.where(ahead == 2, 3, jnp.where(ahead == 3, 2, ahead)) + jnp.where(c // SIDE == core, 0, 4)
    slots = jnp.concatenate([slot, core[None]]).astype(jnp.int32)

    bd = bd_factors.reshape(bd_factors.shape[0], bd_factors.shape[2])
    ints = partial_integrals(slots, bd, ac_factors, swap)
    chip = ints[:4] + permute(ints[4:], 0, "core")
    shard = chip[0] + permute(chip[1], 1, "x", False) + permute(chip[2], -1, "x", False) + permute(chip[3], 2, "x", False)

    arranged = arrange(amplitudes)
    own = lax.dynamic_index_in_dim(arranged, core, 0, False)
    other = permute(lax.dynamic_index_in_dim(arranged, 1 - core, 0, False), 0, "core")

    values = [shard[first:last] for first, last, _ in PARTS]
    values = [gather(v, order_[0], at[order_[0]], sign) for v, (_, _, order_) in zip(values, PARTS)]
    values = [gather(v, order_[1], at[order_[1]], sign) for v, (_, _, order_) in zip(values, PARTS)]
    ups = [permute(v, 1, order_[2]) for v, (_, _, order_) in zip(values, PARTS)]
    downs = [permute(v, -1, order_[2]) for v, (_, _, order_) in zip(values, PARTS)]
    half = [v.shape[0] // 2 for v in values]
    far_up = [permute(v[:h], 1, order_[2]) for v, h, (_, _, order_) in zip(ups, half, PARTS)]
    far_down = [permute(v[h:], -1, order_[2]) for v, h, (_, _, order_) in zip(downs, half, PARTS)]
    pieces, ids = [], []
    for j, (_, _, order_) in enumerate(PARTS):
        pieces += [values[j], ups[j], downs[j], far_up[j], far_down[j]]
        mine = at[order_[2]]
        ids += [4 * j + (mine + s) % SIDE for s in (0, -sign, sign, 2)]
    both = ladder(jnp.stack(ids).astype(jnp.int32), own, other, order, pieces)
    return both[0] + permute(both[1], 0, "core")


def solution(mesh):
    placed = (P("aux", None), P("pair", "aux", None), P(("pair", "aux"), None, None))
    return jax.shard_map(
        body, mesh=mesh, in_specs=placed, out_specs=P(("pair", "aux"), None), check_vma=False
    )
```

```python
import functools

import jax
import jax.numpy as jnp
from jax import lax
from jax.experimental import pallas as pl
from jax.experimental.pallas import tpu as pltpu
from jax.sharding import PartitionSpec as P

AXES = ("pair", "aux")
SIDE = 4
CORES = 2
CHIP_ROWS = 150
FRAME = 152
STEPS = ("yx", "zy", "xz")
WIDE = 2432


def place(z, y, core, x):
    return (((z % SIDE) * SIDE + y % SIDE) * CORES + core) * SIDE + x % SIDE


def permute(value, step, axes):
    pairs = []
    for z in range(SIDE):
        for y in range(SIDE):
            for core in range(CORES):
                for x in range(SIDE):
                    to = dict(z=z, y=y, core=core, x=x)
                    if step:
                        to[axes[core]] += step
                    else:
                        to["core"] = 1 - core
                    pairs.append((place(z, y, core, x), place(**to)))
    return lax.ppermute(value, AXES, pairs)


def where():
    pair = lax.axis_index("pair")
    return pair % CORES, dict(x=lax.axis_index("aux"), y=(pair // CORES) % SIDE, z=pair // (CORES * SIDE))


def reorder(size, across):
    row = lax.broadcasted_iota(jnp.int32, (size, size), 0)
    column = lax.broadcasted_iota(jnp.int32, (size, size), 1)
    return (row % across) * (size // across) + row // across == column


def partial_kernel(first_ref, second_ref, ac_ref, own_ref, other_ref, shifted, products):
    rows = ac_ref.shape[0]
    count_d = first_ref.shape[0]
    group = pl.program_id(0)

    @pl.when(group == 0)
    def _():
        ordered = jnp.dot(ac_ref[...], reorder(128, 8).astype(jnp.bfloat16), preferred_element_type=jnp.float32)
        shifted[...] = jnp.zeros_like(shifted)
        for k in range(4):
            shifted[k, pl.ds((rows * k) % 128, rows), :] = ordered.astype(jnp.bfloat16)

    for k in range(4):
        offset = (rows * k) % 128
        start = rows * k - offset
        length = -(-(offset + rows) // 128) * 128
        for j, bd_ref in enumerate((first_ref, second_ref)):
            products[8 * group + 4 * j + k] = jnp.dot(bd_ref[:, start:start + length], shifted[k, :length, :],
                                                      preferred_element_type=jnp.float32)

    @pl.when(group == pl.num_programs(0) - 1)
    def _():
        core, at = where()
        own_ref[...] = jnp.zeros_like(own_ref)
        other_ref[...] = jnp.zeros_like(other_ref)
        blocks = [products[b] for b in range(16)]
        slabs = [jnp.concatenate([p[:, 16 * c:16 * c + 16] for p in blocks], axis=1) for c in range(8)]
        for which in range(CORES):
            @pl.when(core == which)
            def _():
                for c in range(8):
                    ref = own_ref if c // SIDE == which else other_ref
                    ref[(c - at["x"]) % SIDE, which * count_d:(which + 1) * count_d, :] = slabs[c]


def partial_integrals(bd, ac):
    rows = ac.shape[0]
    out = jax.ShapeDtypeStruct((SIDE, FRAME, 256), jnp.float32)
    whole = pl.BlockSpec(memory_space=pltpu.VMEM)
    return pl.pallas_call(
        partial_kernel,
        grid=(2,),
        out_shape=(out, out),
        in_specs=[pl.BlockSpec((bd.shape[0], 4 * rows), lambda g: (0, 2 * g)),
                  pl.BlockSpec((bd.shape[0], 4 * rows), lambda g: (0, 2 * g + 1)), whole],
        out_specs=(whole, whole),
        scratch_shapes=[pltpu.VMEM((4, -(-(rows + 96) // 128) * 128, 128), jnp.bfloat16),
                        pltpu.VMEM((16, bd.shape[0], 128), jnp.float32)],
        compiler_params=pltpu.CompilerParams(vmem_limit_bytes=48 * 2**20),
        cost_estimate=pl.CostEstimate(flops=10**9, bytes_accessed=8 * 10**6, transcendentals=0),
    )(bd, bd, ac)


def split(value):
    high = value.astype(jnp.bfloat16)
    return high, (value - high.astype(jnp.float32)).astype(jnp.bfloat16)


def arrange_kernel(*refs):
    sources, (high_ref, low_ref, amp, sems) = refs[:-4], refs[-4:]
    step, steps = pl.program_id(0), pl.num_programs(0)
    slots, rows, _, width = amp.shape
    cut = rows // sems.shape[1]
    core, _ = where()

    def each(block, act):
        slot = lax.rem(block, slots)
        first = 0
        for source in sources:
            count = source.shape[0] // rows

            @pl.when(jnp.logical_and(block >= first, block < first + count))
            def _():
                part = source.at[pl.ds((block - first) * rows, rows), pl.ds(SIDE * core, SIDE)]
                for k in range(sems.shape[1]):
                    act(pltpu.make_async_copy(part.at[pl.ds(k * cut, cut)], amp.at[slot, pl.ds(k * cut, cut)],
                                              sems.at[slot, k]))
            first += count

    @pl.when(step == 0)
    def _():
        for block in range(slots - 1):
            each(step + block, lambda copy: copy.start())

    @pl.when(step + slots - 1 < steps)
    def _():
        each(step + slots - 1, lambda copy: copy.start())

    each(step, lambda copy: copy.wait())
    pad = jnp.zeros((rows, WIDE - width), jnp.float32)
    for c in range(SIDE):
        high_ref[c], low_ref[c] = split(jnp.concatenate([amp[lax.rem(step, slots), :, c, :], pad], axis=1))


def arrange(*amps):
    pairs, width = sum(a.shape[0] for a in amps), amps[0].shape[2]
    rows, slots, cuts = 32, 3, 4
    out = jax.ShapeDtypeStruct((SIDE, pairs, WIDE), jnp.bfloat16)
    return pl.pallas_call(
        arrange_kernel,
        grid=(pairs // rows,),
        out_shape=(out, out),
        in_specs=[pl.BlockSpec(memory_space=pl.ANY)] * len(amps),
        out_specs=(pl.BlockSpec((SIDE, rows, WIDE), lambda i: (0, i, 0)),) * 2,
        scratch_shapes=[pltpu.VMEM((slots, rows, SIDE, width), jnp.float32), pltpu.SemaphoreType.DMA((slots, cuts))],
        compiler_params=pltpu.CompilerParams(vmem_limit_bytes=52 * 2**20),
        cost_estimate=pl.CostEstimate(flops=10**6, bytes_accessed=30 * 10**6, transcendentals=0),
    )(*amps)


def product(high, low, matrix):
    mhigh, mlow = split(matrix)
    dot = functools.partial(jnp.dot, preferred_element_type=jnp.float32)
    return dot(high, mhigh) + (dot(high, mlow) + dot(low, mhigh))


def slot(at, coord):
    ahead = (at - coord + SIDE) % SIDE
    return jnp.where(ahead == 0, 0, jnp.where(ahead == SIDE - 1, 1, ahead + 1))


def run_of(c, z, y):
    core, at = where()
    c, z, y = slot(c, at["x"]), slot(z, at["z"]), slot(y, at["y"])
    return jnp.where(core == 0, 16 * c + SIDE * z + y, 16 * z + SIDE * y + c)


def early_kernel(high_ref, low_ref, *refs):
    pieces, out_ref = refs[:6], refs[6]
    blocks, matrix, sems = refs[7:]
    c = pl.program_id(0)

    @pl.when(c == 0)
    def _():
        copies = [pltpu.make_async_copy(piece, blocks.at[pl.ds(8 * k, 8)], sems.at[k]) for k, piece in enumerate(pieces)]
        for copy in copies:
            copy.start()
        out_ref[...] = jnp.zeros_like(out_ref)
        matrix[WIDE - 32:, :] = jnp.zeros((32, 256), jnp.float32)
        blocks[48:] = jnp.zeros((16,) + blocks.shape[1:], jnp.float32)
        for copy in copies:
            copy.wait()

    for z in range(SIDE):
        for y in range(SIDE):
            begin = CHIP_ROWS * (z * SIDE + y)
            matrix[begin:begin + FRAME, :] = blocks[run_of(c, z, y)]
    out_ref[...] += product(high_ref[...], low_ref[...], matrix[...])


def early_ladder(high, low, pieces):
    pairs = high.shape[1]
    amp_spec = pl.BlockSpec((None, pairs, WIDE), lambda c: (c, 0, 0))
    return pl.pallas_call(
        early_kernel,
        grid=(SIDE,),
        in_specs=[amp_spec] * 2 + [pl.BlockSpec(memory_space=pl.ANY)] * len(pieces),
        out_specs=pl.BlockSpec(memory_space=pltpu.VMEM),
        scratch_shapes=[pltpu.VMEM((64, FRAME, 256), jnp.float32), pltpu.VMEM((WIDE, 256), jnp.float32),
                        pltpu.SemaphoreType.DMA((len(pieces),))],
        out_shape=jax.ShapeDtypeStruct((pairs, 256), jnp.float32),
        compiler_params=pltpu.CompilerParams(vmem_limit_bytes=52 * 2**20),
        cost_estimate=pl.CostEstimate(flops=6 * 10**9, bytes_accessed=25 * 10**6, transcendentals=0),
    )(high, low, *pieces)


def late_kernel(high_ref, low_ref, up_ref, down_ref, total_ref, own_ref, other_ref, high, low, matrix, far, sems):
    pairs = total_ref.shape[0] // 2
    core, at = where()
    sources = ((high_ref, high), (low_ref, low))
    size = matrix.shape[0] // SIDE
    matrix[...] = jnp.zeros_like(matrix)
    far[:8] = up_ref[...]
    far[8:] = down_ref[...]

    @pl.when(core == 0)
    def _():
        c = (at["x"] + 2) % SIDE
        copies = [pltpu.make_async_copy(source.at[c], to.at[:, pl.ds(0, WIDE)], sems.at[k])
                  for k, (source, to) in enumerate(sources)]
        for copy in copies:
            copy.start()
        for to in (high, low):
            to[:, WIDE:] = jnp.zeros((2 * pairs, matrix.shape[0] - WIDE), jnp.bfloat16)
        for z in range(SIDE):
            for y in range(SIDE):
                begin = CHIP_ROWS * (z * SIDE + y)
                matrix[begin:begin + FRAME, :] = far[SIDE * slot(z, at["z"]) + slot(y, at["y"])]
        for copy in copies:
            copy.wait()

    @pl.when(core == 1)
    def _():
        z = (at["z"] + 2) % SIDE
        start = jnp.minimum(SIDE * CHIP_ROWS * z // 128, (WIDE - size) // 128) * 128
        copies = [pltpu.make_async_copy(source.at[c, :, pl.ds(pl.multiple_of(start, 128), size)],
                                        to.at[:, pl.ds(size * c, size)], sems.at[2 * c + k])
                  for c in range(SIDE) for k, (source, to) in enumerate(sources)]
        for copy in copies:
            copy.start()
        for which in range(SIDE):
            @pl.when(z == which)
            def _():
                first = SIDE * CHIP_ROWS * which
                offset = first - min(first // 128, (WIDE - size) // 128) * 128
                for c in range(SIDE):
                    for y in range(SIDE):
                        to = size * c + offset + CHIP_ROWS * y
                        matrix[to:to + FRAME, :] = far[SIDE * slot(y, at["y"]) + slot(c, at["x"])]
        for copy in copies:
            copy.wait()

    result = jnp.dot(total_ref[...] + product(high[...], low[...], matrix[...]),
                     reorder(256, 16).astype(jnp.float32), precision=lax.Precision.HIGHEST,
                     preferred_element_type=jnp.float32)
    own_ref[...] = result[:pairs]
    other_ref[...] = result[pairs:]


def late_ladder(high, low, up, down, total):
    pairs = high.shape[1] // 2
    out = jax.ShapeDtypeStruct((pairs, 256), jnp.float32)
    whole = pl.BlockSpec(memory_space=pltpu.VMEM)
    wide = SIDE * 768
    return pl.pallas_call(
        late_kernel,
        in_specs=[pl.BlockSpec(memory_space=pl.ANY)] * 2 + [whole] * 3,
        out_specs=(whole, whole),
        scratch_shapes=[pltpu.VMEM((2 * pairs, wide), jnp.bfloat16)] * 2 + [
            pltpu.VMEM((wide, 256), jnp.float32), pltpu.VMEM((16,) + up.shape[1:], jnp.float32),
            pltpu.SemaphoreType.DMA((8,))],
        out_shape=(out, out),
        compiler_params=pltpu.CompilerParams(vmem_limit_bytes=40 * 2**20),
        cost_estimate=pl.CostEstimate(flops=2 * 10**9, bytes_accessed=8 * 10**6, transcendentals=0),
    )(high, low, up, down, total)


def fetch(value, axes):
    far = permute(value, 2, axes)
    return [value, permute(value, 1, axes), permute(value, -1, axes), far]


def body(ac_factors, bd_factors, amplitudes):
    barrier = lax.optimization_barrier
    bd = bd_factors.reshape(bd_factors.shape[0], bd_factors.shape[2])
    mine, sent = partial_integrals(bd, ac_factors)
    chip = mine + permute(sent, 0, None)
    amplitudes, chip = barrier((amplitudes, chip))
    other = permute(amplitudes, 0, None)
    shard = chip[0] + permute(chip[2], 2, "xx") + permute(chip[1], 1, "xx") + permute(chip[3], -1, "xx")

    line = jnp.concatenate(fetch(shard, STEPS[0]), axis=0)
    plane = fetch(line, STEPS[1])
    first, second = jnp.concatenate(plane[:2], axis=0), jnp.concatenate(plane[2:], axis=0)
    first, second, amplitudes, other = barrier((first, second, amplitudes, other))
    up_first, down_second = permute(first, 1, STEPS[2]), permute(second, -1, STEPS[2])
    up_second, down_first = permute(second, 1, STEPS[2]), permute(first, -1, STEPS[2])
    high, low = arrange(amplitudes, other)
    up_first, down_second, high, low = barrier((up_first, down_second, high, low))
    far_up, far_down = permute(up_first, 1, STEPS[2]), permute(down_second, -1, STEPS[2])

    def runs(value):
        return value.reshape(-1, FRAME, 256)

    total = early_ladder(high, low, [runs(v) for v in (first, second, up_first, up_second, down_first, down_second)])
    kept, given = late_ladder(high, low, runs(far_up), runs(far_down), total)
    return kept + permute(given, 0, None)


def solution(mesh):
    placed = (P("aux", None), P("pair", "aux", None), P(("pair", "aux"), None, None))
    return jax.shard_map(
        body, mesh=mesh, in_specs=placed, out_specs=P(("pair", "aux"), None), check_vma=False
    )
```

```python
import functools

import jax
import jax.numpy as jnp
from jax import lax
from jax.experimental import pallas as pl
from jax.experimental.pallas import tpu as pltpu
from jax.sharding import PartitionSpec as P

AXES = ("pair", "aux")
SIDE = 4
CORES = 2
CHIP_ROWS = 150
FRAME = 152
STEPS = ("yx", "zy", "xz")
WINDOW = 768
WIDE = 2432


def place(z, y, core, x):
    return (((z % SIDE) * SIDE + y % SIDE) * CORES + core) * SIDE + x % SIDE


def permute(value, step, axes):
    pairs = []
    for z in range(SIDE):
        for y in range(SIDE):
            for core in range(CORES):
                for x in range(SIDE):
                    to = dict(z=z, y=y, core=core, x=x)
                    if step:
                        to[axes[core]] += step
                    else:
                        to["core"] = 1 - core
                    pairs.append((place(z, y, core, x), place(**to)))
    return lax.ppermute(value, AXES, pairs)


def where():
    pair = lax.axis_index("pair")
    return pair % CORES, dict(x=lax.axis_index("aux"), y=(pair // CORES) % SIDE, z=pair // (CORES * SIDE))


def reorder(size, across):
    row = lax.broadcasted_iota(jnp.int32, (size, size), 0)
    column = lax.broadcasted_iota(jnp.int32, (size, size), 1)
    return (row % across) * (size // across) + row // across == column


def partial_kernel(first_ref, second_ref, ac_ref, own_ref, other_ref, shifted, products):
    rows = ac_ref.shape[0]
    count_d = products.shape[1]
    group = pl.program_id(0)

    @pl.when(group == 0)
    def _():
        ordered = jnp.dot(ac_ref[...], reorder(128, 8).astype(jnp.bfloat16), preferred_element_type=jnp.float32)
        shifted[...] = jnp.zeros_like(shifted)
        for k in range(4):
            shifted[k, pl.ds((rows * k) % 128, rows), :] = ordered.astype(jnp.bfloat16)

    height = first_ref.shape[0]
    for k in range(4):
        offset = (rows * k) % 128
        start = rows * k - offset
        length = -(-(offset + rows) // 128) * 128
        both = jnp.concatenate([ref[:, start:start + length] for ref in (first_ref, second_ref)], axis=0)
        both = jnp.dot(both, shifted[k, :length, :], preferred_element_type=jnp.float32)
        products[8 * group + k] = both[:count_d]
        products[8 * group + 4 + k] = both[height:height + count_d]

    @pl.when(group == pl.num_programs(0) - 1)
    def _():
        core, at = where()
        own_ref[...] = jnp.zeros_like(own_ref)
        other_ref[...] = jnp.zeros_like(other_ref)
        column = lax.broadcasted_iota(jnp.int32, (count_d, 128), 1) // 16
        turned = [pltpu.roll(products[b], 16 * (b % 8), axis=1) if b % 8 else products[b] for b in range(16)]
        slabs = []
        for c in range(8):
            sides = []
            for side in (turned[:8], turned[8:]):
                picked = side[0]
                for b in range(1, 8):
                    picked = jnp.where(column == (c + b) % 8, side[b], picked)
                sides.append(pltpu.roll(picked, 128 - 16 * c, axis=1) if c else picked)
            slabs.append(jnp.concatenate(sides, axis=1))
        for which in range(CORES):
            @pl.when(core == which)
            def _():
                for c in range(8):
                    ref = own_ref if c // SIDE == which else other_ref
                    ref[(c - at["x"]) % SIDE, which * count_d:(which + 1) * count_d, :] = slabs[c]


def partial_integrals(bd, ac):
    rows = ac.shape[0]
    height = -(-bd.shape[0] // 16) * 16
    out = jax.ShapeDtypeStruct((SIDE, FRAME, 256), jnp.float32)
    whole = pl.BlockSpec(memory_space=pltpu.VMEM)
    return pl.pallas_call(
        partial_kernel,
        grid=(2,),
        out_shape=(out, out),
        in_specs=[pl.BlockSpec((height, 4 * rows), lambda g: (0, 2 * g)),
                  pl.BlockSpec((height, 4 * rows), lambda g: (0, 2 * g + 1)), whole],
        out_specs=(whole, whole),
        scratch_shapes=[pltpu.VMEM((4, -(-(rows + 96) // 128) * 128, 128), jnp.bfloat16),
                        pltpu.VMEM((16, bd.shape[0], 128), jnp.float32)],
        compiler_params=pltpu.CompilerParams(vmem_limit_bytes=48 * 2**20),
        cost_estimate=pl.CostEstimate(flops=10**9, bytes_accessed=8 * 10**6, transcendentals=0),
    )(bd, bd, ac)


def split(value):
    high = value.astype(jnp.bfloat16)
    return high, (value - high.astype(jnp.float32)).astype(jnp.bfloat16)


def arrange_kernel(amp_ref, high_ref, low_ref, amp, sems):
    step, steps = pl.program_id(0), pl.num_programs(0)
    slots, rows, _, width = amp.shape
    cut = rows // sems.shape[1]
    core, _ = where()

    def fetch(block):
        source = amp_ref.at[pl.ds(block * rows, rows), pl.ds(SIDE * core, SIDE)]
        slot = lax.rem(block, slots)
        return [pltpu.make_async_copy(source.at[pl.ds(k * cut, cut)], amp.at[slot, pl.ds(k * cut, cut)], sems.at[slot, k])
                for k in range(sems.shape[1])]

    @pl.when(step == 0)
    def _():
        for block in range(slots - 1):
            for copy in fetch(step + block):
                copy.start()

    @pl.when(step + slots - 1 < steps)
    def _():
        for copy in fetch(step + slots - 1):
            copy.start()

    for copy in fetch(step):
        copy.wait()
    pad = jnp.zeros((rows, WIDE - width), jnp.float32)
    for c in range(SIDE):
        high_ref[c], low_ref[c] = split(jnp.concatenate([amp[lax.rem(step, slots), :, c, :], pad], axis=1))


def arrange(amps, room):
    pairs, _, width = amps.shape
    rows, slots, cuts = 32, 3, 4
    out = jax.ShapeDtypeStruct((SIDE, pairs, WIDE), jnp.bfloat16)
    return pl.pallas_call(
        arrange_kernel,
        grid=(pairs // rows,),
        out_shape=(out, out),
        in_specs=[pl.BlockSpec(memory_space=pl.ANY)],
        out_specs=(pl.BlockSpec((SIDE, rows, WIDE), lambda i: (0, i, 0)),) * 2,
        scratch_shapes=[pltpu.VMEM((slots, rows, SIDE, width), jnp.float32), pltpu.SemaphoreType.DMA((slots, cuts))],
        compiler_params=pltpu.CompilerParams(vmem_limit_bytes=room * 2**20),
        cost_estimate=pl.CostEstimate(flops=10**6, bytes_accessed=15 * 10**6, transcendentals=0),
    )(amps)


def product(high, low, matrix):
    mhigh, mlow = split(matrix)
    dot = functools.partial(jnp.dot, preferred_element_type=jnp.float32)
    return dot(high, mhigh) + (dot(high, mlow) + dot(low, mhigh))


def slot(at, coord):
    ahead = (at - coord + SIDE) % SIDE
    return jnp.where(ahead == 0, 0, jnp.where(ahead == SIDE - 1, 1, ahead + 1))


def run_of(c, z, y):
    core, at = where()
    c, z, y = slot(c, at["x"]), slot(z, at["z"]), slot(y, at["y"])
    return jnp.where(core == 0, 16 * c + SIDE * z + y, 16 * z + SIDE * y + c)


def early_kernel(own_high, own_low, other_high, other_low, *refs):
    pieces, (out_ref, far_high, far_low, blocks, matrix, sems) = refs[:-6], refs[-6:]
    c = pl.program_id(0)

    @pl.when(c == 0)
    def _():
        copies, filled = [], 0
        for k, piece in enumerate(pieces):
            copies.append(pltpu.make_async_copy(piece, blocks.at[pl.ds(filled, piece.shape[0])], sems.at[k]))
            filled += piece.shape[0]
        for copy in copies:
            copy.start()
        out_ref[...] = jnp.zeros_like(out_ref)
        matrix[WIDE - 32:, :] = jnp.zeros((32, 256), jnp.float32)
        blocks[48:] = jnp.zeros((16,) + blocks.shape[1:], jnp.float32)
        for copy in copies:
            copy.wait()

    for z in range(SIDE):
        for y in range(SIDE):
            begin = CHIP_ROWS * (z * SIDE + y)
            matrix[begin:begin + FRAME, :] = blocks[run_of(c, z, y)]
    high = jnp.concatenate([own_high[...], other_high[...]], axis=0)
    low = jnp.concatenate([own_low[...], other_low[...]], axis=0)
    out_ref[...] += product(high, low, matrix[...])

    core, at = where()
    size = far_high.shape[1] // SIDE

    @pl.when(jnp.logical_and(core == 0, (at["x"] + 2) % SIDE == c))
    def _():
        for to, (one, two) in ((far_high, (own_high, other_high)), (far_low, (own_low, other_low))):
            to[:, :WIDE] = jnp.concatenate([one[...], two[...]], axis=0)
            to[:, WIDE:] = jnp.zeros((to.shape[0], SIDE * size - WIDE), jnp.bfloat16)

    @pl.when(core == 1)
    def _():
        start = jnp.minimum(SIDE * CHIP_ROWS * ((at["z"] + 2) % SIDE) // 128, (WIDE - size) // 128) * 128
        window = pl.ds(pl.multiple_of(start, 128), size)
        for to, (one, two) in ((far_high, (own_high, other_high)), (far_low, (own_low, other_low))):
            to[:, pl.ds(pl.multiple_of(size * c, 128), size)] = jnp.concatenate([one[:, window], two[:, window]], axis=0)


def early_ladder(own, other, pieces):
    pairs = own[0].shape[1]
    amp_spec = pl.BlockSpec((None, pairs, WIDE), lambda c: (c, 0, 0))
    far = jax.ShapeDtypeStruct((2 * pairs, SIDE * WINDOW), jnp.bfloat16)
    return pl.pallas_call(
        early_kernel,
        grid=(SIDE,),
        in_specs=[amp_spec] * 4 + [pl.BlockSpec(memory_space=pl.ANY)] * len(pieces),
        out_specs=(pl.BlockSpec(memory_space=pltpu.VMEM),) * 3,
        scratch_shapes=[pltpu.VMEM((64, FRAME, 256), jnp.float32), pltpu.VMEM((WIDE, 256), jnp.float32),
                        pltpu.SemaphoreType.DMA((len(pieces),))],
        out_shape=(jax.ShapeDtypeStruct((2 * pairs, 256), jnp.float32), far, far),
        compiler_params=pltpu.CompilerParams(vmem_limit_bytes=30 * 2**20),
        cost_estimate=pl.CostEstimate(flops=6 * 10**9, bytes_accessed=25 * 10**6, transcendentals=0),
    )(*own, *other, *pieces)


def late_kernel(high_ref, low_ref, up_ref, near_ref, far_ref, total_ref, own_ref, other_ref, matrix, far):
    pairs = total_ref.shape[0] // 2
    core, at = where()
    matrix[...] = jnp.zeros_like(matrix)
    far[:8] = up_ref[...]
    far[8:12] = near_ref[...]
    far[12:] = far_ref[...]

    @pl.when(core == 0)
    def _():
        for z in range(SIDE):
            for y in range(SIDE):
                begin = CHIP_ROWS * (z * SIDE + y)
                matrix[begin:begin + FRAME, :] = far[SIDE * slot(z, at["z"]) + slot(y, at["y"])]

    for z in range(SIDE):
        @pl.when(jnp.logical_and(core == 1, (at["z"] + 2) % SIDE == z))
        def _():
            first = SIDE * CHIP_ROWS * z
            offset = first - min(first // 128, (WIDE - WINDOW) // 128) * 128
            for c in range(SIDE):
                for y in range(SIDE):
                    to = WINDOW * c + offset + CHIP_ROWS * y
                    matrix[to:to + FRAME, :] = far[SIDE * slot(y, at["y"]) + slot(c, at["x"])]

    result = jnp.dot(total_ref[...] + product(high_ref[...], low_ref[...], matrix[...]),
                     reorder(256, 16).astype(jnp.float32), precision=lax.Precision.HIGHEST,
                     preferred_element_type=jnp.float32)
    own_ref[...] = result[:pairs]
    other_ref[...] = result[pairs:]


def late_ladder(high, low, pieces, total):
    out = jax.ShapeDtypeStruct((total.shape[0] // 2, 256), jnp.float32)
    whole = pl.BlockSpec(memory_space=pltpu.VMEM)
    return pl.pallas_call(
        late_kernel,
        in_specs=[whole] * (3 + len(pieces)),
        out_specs=(whole, whole),
        scratch_shapes=[pltpu.VMEM((SIDE * WINDOW, 256), jnp.float32), pltpu.VMEM((16, FRAME, 256), jnp.float32)],
        out_shape=(out, out),
        compiler_params=pltpu.CompilerParams(vmem_limit_bytes=32 * 2**20),
        cost_estimate=pl.CostEstimate(flops=2 * 10**9, bytes_accessed=8 * 10**6, transcendentals=0),
    )(high, low, *pieces, total)


def fetch(value, axes):
    far = permute(value, 2, axes)
    return [value, permute(value, 1, axes), permute(value, -1, axes), far]


def body(ac_factors, bd_factors, amplitudes):
    barrier = lax.optimization_barrier
    bd = bd_factors.reshape(bd_factors.shape[0], bd_factors.shape[2])
    mine, sent = partial_integrals(bd, ac_factors)
    chip = mine + permute(sent, 0, None)
    amplitudes, chip = barrier((amplitudes, chip))
    other = permute(amplitudes, 0, None)
    own = arrange(amplitudes, 44)
    shard = chip[0] + permute(chip[1], 1, "xx") + permute(chip[3], -1, "xx") + permute(chip[2], 2, "xx")

    shard, own = barrier((shard, own))
    line, other = barrier((fetch(shard, STEPS[0]), other))
    halves = [jnp.concatenate(part, axis=0) for part in (line[:2], line[2:])]
    up = [permute(half, 1, STEPS[1]) for half in halves]
    down = [permute(half, -1, STEPS[1]) for half in halves]
    far = [permute(up[0], 1, STEPS[1]), permute(down[1], -1, STEPS[1])]
    first, near = jnp.concatenate(halves + up, axis=0), jnp.concatenate(down, axis=0)
    up_first, down_near = permute(first, 1, STEPS[2]), permute(near, -1, STEPS[2])
    far, other = barrier((far, other))
    far = jnp.concatenate(far, axis=0)
    second = jnp.concatenate([near, far], axis=0)
    down_far = permute(far, -1, STEPS[2])
    up_second, down_first = permute(second, 1, STEPS[2]), permute(first, -1, STEPS[2])
    other = arrange(other, 16)
    up_first, other = barrier((up_first, other))
    far_up = permute(up_first, 1, STEPS[2])
    up_first, down_near = barrier((up_first, down_near))
    far_down = [permute(down_near, -1, STEPS[2]), permute(down_far, -1, STEPS[2])]

    def runs(value):
        return value.reshape(-1, FRAME, 256)

    pieces = (first, second, up_first, up_second, down_first, down_near, down_far)
    total, high, low = early_ladder(own, other, [runs(v) for v in pieces])
    kept, given = late_ladder(high, low, [runs(v) for v in [far_up] + far_down], total)
    return kept + permute(given, 0, None)


def solution(mesh):
    placed = (P("aux", None), P("pair", "aux", None), P(("pair", "aux"), None, None))
    return jax.shard_map(
        body, mesh=mesh, in_specs=placed, out_specs=P(("pair", "aux"), None), check_vma=False
    )
```

```python
import functools

import jax
import jax.numpy as jnp
from jax import lax
from jax.experimental import pallas as pl
from jax.experimental.pallas import tpu as pltpu
from jax.sharding import PartitionSpec as P

AXES = ("pair", "aux")
SIDE = 4
CORES = 2
CHIP_ROWS = 150
FRAME = 152
STEPS = ("yx", "zy", "xz")
WINDOW = 768
WIDE = 2432


def place(z, y, core, x):
    return (((z % SIDE) * SIDE + y % SIDE) * CORES + core) * SIDE + x % SIDE


def permute(value, step, axes):
    pairs = []
    for z in range(SIDE):
        for y in range(SIDE):
            for core in range(CORES):
                for x in range(SIDE):
                    to = dict(z=z, y=y, core=core, x=x)
                    if step:
                        to[axes[core]] += step
                    else:
                        to["core"] = 1 - core
                    pairs.append((place(z, y, core, x), place(**to)))
    return lax.ppermute(value, AXES, pairs)


def where():
    pair = lax.axis_index("pair")
    return pair % CORES, dict(x=lax.axis_index("aux"), y=(pair // CORES) % SIDE, z=pair // (CORES * SIDE))


def reorder(size, across):
    row = lax.broadcasted_iota(jnp.int32, (size, size), 0)
    column = lax.broadcasted_iota(jnp.int32, (size, size), 1)
    return (row % across) * (size // across) + row // across == column


def partial_kernel(first_ref, second_ref, ac_ref, own_ref, other_ref, shifted, products):
    rows = ac_ref.shape[0]
    count_d = products.shape[1]
    group = pl.program_id(0)

    @pl.when(group == 0)
    def _():
        ordered = jnp.dot(ac_ref[...], reorder(128, 8).astype(jnp.bfloat16), preferred_element_type=jnp.float32)
        shifted[...] = jnp.zeros_like(shifted)
        for k in range(4):
            shifted[k, pl.ds((rows * k) % 128, rows), :] = ordered.astype(jnp.bfloat16)

    height = first_ref.shape[0]
    for k in range(4):
        offset = (rows * k) % 128
        start = rows * k - offset
        length = -(-(offset + rows) // 128) * 128
        both = jnp.concatenate([ref[:, start:start + length] for ref in (first_ref, second_ref)], axis=0)
        both = jnp.dot(both, shifted[k, :length, :], preferred_element_type=jnp.float32)
        products[8 * group + k] = both[:count_d]
        products[8 * group + 4 + k] = both[height:height + count_d]

    @pl.when(group == pl.num_programs(0) - 1)
    def _():
        core, at = where()
        own_ref[...] = jnp.zeros_like(own_ref)
        other_ref[...] = jnp.zeros_like(other_ref)
        column = lax.broadcasted_iota(jnp.int32, (count_d, 128), 1) // 16
        turned = [pltpu.roll(products[b], 16 * (b % 8), axis=1) if b % 8 else products[b] for b in range(16)]
        slabs = []
        for c in range(8):
            sides = []
            for side in (turned[:8], turned[8:]):
                picked = side[0]
                for b in range(1, 8):
                    picked = jnp.where(column == (c + b) % 8, side[b], picked)
                sides.append(pltpu.roll(picked, 128 - 16 * c, axis=1) if c else picked)
            slabs.append(jnp.concatenate(sides, axis=1))
        for which in range(CORES):
            @pl.when(core == which)
            def _():
                for c in range(8):
                    ref = own_ref if c // SIDE == which else other_ref
                    ref[(c - at["x"]) % SIDE, which * count_d:(which + 1) * count_d, :] = slabs[c]


def partial_integrals(bd, ac):
    rows = ac.shape[0]
    height = -(-bd.shape[0] // 16) * 16
    out = jax.ShapeDtypeStruct((SIDE, FRAME, 256), jnp.float32)
    whole = pl.BlockSpec(memory_space=pltpu.VMEM)
    return pl.pallas_call(
        partial_kernel,
        grid=(2,),
        out_shape=(out, out),
        in_specs=[pl.BlockSpec((height, 4 * rows), lambda g: (0, 2 * g)),
                  pl.BlockSpec((height, 4 * rows), lambda g: (0, 2 * g + 1)),
                  pl.BlockSpec(ac.shape, lambda g: (0, 0))],
        out_specs=(whole, whole),
        scratch_shapes=[pltpu.VMEM((4, -(-(rows + 96) // 128) * 128, 128), jnp.bfloat16),
                        pltpu.VMEM((16, bd.shape[0], 128), jnp.float32)],
        compiler_params=pltpu.CompilerParams(vmem_limit_bytes=48 * 2**20),
        cost_estimate=pl.CostEstimate(flops=10**9, bytes_accessed=8 * 10**6, transcendentals=0),
    )(bd, bd, ac)


def split(value):
    high = value.astype(jnp.bfloat16)
    return high, (value - high.astype(jnp.float32)).astype(jnp.bfloat16)


def arrange_kernel(amp_ref, high_ref, low_ref, amp, sems):
    step, steps = pl.program_id(0), pl.num_programs(0)
    slots, rows, _, width = amp.shape
    cut = rows // sems.shape[1]
    core, _ = where()

    def fetch(block):
        source = amp_ref.at[pl.ds(block * rows, rows), pl.ds(SIDE * core, SIDE)]
        slot = lax.rem(block, slots)
        return [pltpu.make_async_copy(source.at[pl.ds(k * cut, cut)], amp.at[slot, pl.ds(k * cut, cut)], sems.at[slot, k])
                for k in range(sems.shape[1])]

    @pl.when(step == 0)
    def _():
        for block in range(slots - 1):
            for copy in fetch(step + block):
                copy.start()

    @pl.when(step + slots - 1 < steps)
    def _():
        for copy in fetch(step + slots - 1):
            copy.start()

    for copy in fetch(step):
        copy.wait()
    pad = jnp.zeros((rows, WIDE - width), jnp.float32)
    for c in range(SIDE):
        high_ref[c], low_ref[c] = split(jnp.concatenate([amp[lax.rem(step, slots), :, c, :], pad], axis=1))


def arrange(amps, room):
    pairs, _, width = amps.shape
    rows, slots, cuts = 32, 3, 4
    out = jax.ShapeDtypeStruct((SIDE, pairs, WIDE), jnp.bfloat16)
    return pl.pallas_call(
        arrange_kernel,
        grid=(pairs // rows,),
        out_shape=(out, out),
        in_specs=[pl.BlockSpec(memory_space=pl.ANY)],
        out_specs=(pl.BlockSpec((SIDE, rows, WIDE), lambda i: (0, i, 0)),) * 2,
        scratch_shapes=[pltpu.VMEM((slots, rows, SIDE, width), jnp.float32), pltpu.SemaphoreType.DMA((slots, cuts))],
        compiler_params=pltpu.CompilerParams(vmem_limit_bytes=room * 2**20),
        cost_estimate=pl.CostEstimate(flops=10**6, bytes_accessed=15 * 10**6, transcendentals=0),
    )(amps)


def product(high, low, matrix):
    mhigh, mlow = split(matrix)
    dot = functools.partial(jnp.dot, preferred_element_type=jnp.float32)
    return dot(high, mhigh) + (dot(high, mlow) + dot(low, mhigh))


def slot(at, coord):
    ahead = (at - coord + SIDE) % SIDE
    return jnp.where(ahead == 0, 0, jnp.where(ahead == SIDE - 1, 1, ahead + 1))


def run_of(c, z, y):
    core, at = where()
    c, z, y = slot(c, at["x"]), slot(z, at["z"]), slot(y, at["y"])
    return jnp.where(core == 0, 16 * c + SIDE * z + y, 16 * z + SIDE * y + c)


def early_kernel(own_high, own_low, other_high, other_low, *refs):
    pieces, (out_ref, far_high, far_low, blocks, matrix, sems) = refs[:-6], refs[-6:]
    c = pl.program_id(0)

    @pl.when(c == 0)
    def _():
        copies, filled = [], 0
        for k, piece in enumerate(pieces):
            copies.append(pltpu.make_async_copy(piece, blocks.at[pl.ds(filled, piece.shape[0])], sems.at[k]))
            filled += piece.shape[0]
        for copy in copies:
            copy.start()
        out_ref[...] = jnp.zeros_like(out_ref)
        matrix[WIDE - 32:, :] = jnp.zeros((32, 256), jnp.float32)
        blocks[48:] = jnp.zeros((16,) + blocks.shape[1:], jnp.float32)
        for copy in copies:
            copy.wait()

    for z in range(SIDE):
        for y in range(SIDE):
            begin = CHIP_ROWS * (z * SIDE + y)
            matrix[begin:begin + FRAME, :] = blocks[run_of(c, z, y)]
    high = jnp.concatenate([own_high[...], other_high[...]], axis=0)
    low = jnp.concatenate([own_low[...], other_low[...]], axis=0)
    out_ref[...] += product(high, low, matrix[...])

    core, at = where()
    size = far_high.shape[1] // SIDE

    @pl.when(jnp.logical_and(core == 0, (at["x"] + 2) % SIDE == c))
    def _():
        for to, (one, two) in ((far_high, (own_high, other_high)), (far_low, (own_low, other_low))):
            to[:, :WIDE] = jnp.concatenate([one[...], two[...]], axis=0)
            to[:, WIDE:] = jnp.zeros((to.shape[0], SIDE * size - WIDE), jnp.bfloat16)

    @pl.when(core == 1)
    def _():
        start = jnp.minimum(SIDE * CHIP_ROWS * ((at["z"] + 2) % SIDE) // 128, (WIDE - size) // 128) * 128
        window = pl.ds(pl.multiple_of(start, 128), size)
        for to, (one, two) in ((far_high, (own_high, other_high)), (far_low, (own_low, other_low))):
            to[:, pl.ds(pl.multiple_of(size * c, 128), size)] = jnp.concatenate([one[:, window], two[:, window]], axis=0)


def early_ladder(own, other, pieces):
    pairs = own[0].shape[1]
    amp_spec = pl.BlockSpec((None, pairs, WIDE), lambda c: (c, 0, 0))
    far = jax.ShapeDtypeStruct((2 * pairs, SIDE * WINDOW), jnp.bfloat16)
    return pl.pallas_call(
        early_kernel,
        grid=(SIDE,),
        in_specs=[amp_spec] * 4 + [pl.BlockSpec(memory_space=pl.ANY)] * len(pieces),
        out_specs=(pl.BlockSpec(memory_space=pltpu.VMEM),) * 3,
        scratch_shapes=[pltpu.VMEM((64, FRAME, 256), jnp.float32), pltpu.VMEM((WIDE, 256), jnp.float32),
                        pltpu.SemaphoreType.DMA((len(pieces),))],
        out_shape=(jax.ShapeDtypeStruct((2 * pairs, 256), jnp.float32), far, far),
        compiler_params=pltpu.CompilerParams(vmem_limit_bytes=30 * 2**20),
        cost_estimate=pl.CostEstimate(flops=6 * 10**9, bytes_accessed=25 * 10**6, transcendentals=0),
    )(*own, *other, *pieces)


def late_kernel(high_ref, low_ref, up_ref, near_ref, far_ref, total_ref, own_ref, other_ref, matrix, far):
    pairs = total_ref.shape[0] // 2
    core, at = where()
    matrix[...] = jnp.zeros_like(matrix)
    far[:8] = up_ref[...]
    far[8:12] = near_ref[...]
    far[12:] = far_ref[...]

    @pl.when(core == 0)
    def _():
        for z in range(SIDE):
            for y in range(SIDE):
                begin = CHIP_ROWS * (z * SIDE + y)
                matrix[begin:begin + FRAME, :] = far[SIDE * slot(z, at["z"]) + slot(y, at["y"])]

    for z in range(SIDE):
        @pl.when(jnp.logical_and(core == 1, (at["z"] + 2) % SIDE == z))
        def _():
            first = SIDE * CHIP_ROWS * z
            offset = first - min(first // 128, (WIDE - WINDOW) // 128) * 128
            for c in range(SIDE):
                for y in range(SIDE):
                    to = WINDOW * c + offset + CHIP_ROWS * y
                    matrix[to:to + FRAME, :] = far[SIDE * slot(y, at["y"]) + slot(c, at["x"])]

    result = jnp.dot(total_ref[...] + product(high_ref[...], low_ref[...], matrix[...]),
                     reorder(256, 16).astype(jnp.float32), precision=lax.Precision.HIGHEST,
                     preferred_element_type=jnp.float32)
    own_ref[...] = result[:pairs]
    other_ref[...] = result[pairs:]


def late_ladder(high, low, pieces, total):
    out = jax.ShapeDtypeStruct((total.shape[0] // 2, 256), jnp.float32)
    whole = pl.BlockSpec(memory_space=pltpu.VMEM)
    return pl.pallas_call(
        late_kernel,
        in_specs=[whole] * (3 + len(pieces)),
        out_specs=(whole, whole),
        scratch_shapes=[pltpu.VMEM((SIDE * WINDOW, 256), jnp.float32), pltpu.VMEM((16, FRAME, 256), jnp.float32)],
        out_shape=(out, out),
        compiler_params=pltpu.CompilerParams(vmem_limit_bytes=32 * 2**20),
        cost_estimate=pl.CostEstimate(flops=2 * 10**9, bytes_accessed=8 * 10**6, transcendentals=0),
    )(high, low, *pieces, total)


def fetch(value, axes):
    far = permute(value, 2, axes)
    return [value, permute(value, 1, axes), permute(value, -1, axes), far]


def body(ac_factors, bd_factors, amplitudes):
    barrier = lax.optimization_barrier
    bd = bd_factors.reshape(bd_factors.shape[0], bd_factors.shape[2])
    mine, sent = partial_integrals(bd, ac_factors)
    chip = mine + permute(sent, 0, None)
    amplitudes, chip = barrier((amplitudes, chip))
    other = permute(amplitudes, 0, None)
    own = arrange(amplitudes, 44)
    shard = chip[0] + permute(chip[1], 1, "xx") + permute(chip[3], -1, "xx") + permute(chip[2], 2, "xx")

    shard, own = barrier((shard, own))
    line, other = barrier((fetch(shard, STEPS[0]), other))
    halves = [jnp.concatenate(part, axis=0) for part in (line[:2], line[2:])]
    up = [permute(half, 1, STEPS[1]) for half in halves]
    down = [permute(half, -1, STEPS[1]) for half in halves]
    far = [permute(up[0], 1, STEPS[1]), permute(down[1], -1, STEPS[1])]
    first, near = jnp.concatenate(halves + up, axis=0), jnp.concatenate(down, axis=0)
    up_first, down_near = permute(first, 1, STEPS[2]), permute(near, -1, STEPS[2])
    far, other = barrier((far, other))
    far = jnp.concatenate(far, axis=0)
    second = jnp.concatenate([near, far], axis=0)
    down_far = permute(far, -1, STEPS[2])
    up_second, down_first = permute(second, 1, STEPS[2]), permute(first, -1, STEPS[2])
    other = arrange(other, 16)
    up_first, other = barrier((up_first, other))
    far_up = permute(up_first, 1, STEPS[2])
    up_first, down_far = barrier((up_first, down_far))
    far_far = permute(down_far, -1, STEPS[2])
    down_near, down_first, up_second = barrier((down_near, down_first, up_second))
    far_down = [permute(down_near, -1, STEPS[2]), far_far]

    def runs(value):
        return value.reshape(-1, FRAME, 256)

    pieces = (first, second, up_first, up_second, down_first, down_near, down_far)
    total, high, low = early_ladder(own, other, [runs(v) for v in pieces])
    kept, given = late_ladder(high, low, [runs(v) for v in [far_up] + far_down], total)
    return kept + permute(given, 0, None)


def solution(mesh):
    placed = (P("aux", None), P("pair", "aux", None), P(("pair", "aux"), None, None))
    return jax.shard_map(
        body, mesh=mesh, in_specs=placed, out_specs=P(("pair", "aux"), None), check_vma=False
    )
```

```python
import functools

import jax
import jax.numpy as jnp
from jax import lax
from jax.experimental import pallas as pl
from jax.experimental.pallas import tpu as pltpu
from jax.sharding import PartitionSpec as P

AXES = ("pair", "aux")
SIDE = 4
CORES = 2
CHIP_ROWS = 150
FRAME = 152
STEPS = ("yx", "zy", "xz")
WINDOW = 768
WIDE = 2432


def place(z, y, core, x):
    return (((z % SIDE) * SIDE + y % SIDE) * CORES + core) * SIDE + x % SIDE


def permute(value, step, axes):
    pairs = []
    for z in range(SIDE):
        for y in range(SIDE):
            for core in range(CORES):
                for x in range(SIDE):
                    to = dict(z=z, y=y, core=core, x=x)
                    if step:
                        to[axes[core]] += step
                    else:
                        to["core"] = 1 - core
                    pairs.append((place(z, y, core, x), place(**to)))
    return lax.ppermute(value, AXES, pairs)


def where():
    pair = lax.axis_index("pair")
    return pair % CORES, dict(x=lax.axis_index("aux"), y=(pair // CORES) % SIDE, z=pair // (CORES * SIDE))


def reorder(size, across):
    row = lax.broadcasted_iota(jnp.int32, (size, size), 0)
    column = lax.broadcasted_iota(jnp.int32, (size, size), 1)
    return (row % across) * (size // across) + row // across == column


def partial_kernel(first_ref, second_ref, ac_ref, own_ref, other_ref, shifted, products):
    rows = ac_ref.shape[0]
    count_d = products.shape[1]
    group = pl.program_id(0)

    @pl.when(group == 0)
    def _():
        ordered = jnp.dot(ac_ref[...], reorder(128, 8).astype(jnp.bfloat16), preferred_element_type=jnp.float32)
        shifted[...] = jnp.zeros_like(shifted)
        for k in range(4):
            shifted[k, pl.ds((rows * k) % 128, rows), :] = ordered.astype(jnp.bfloat16)

    for k in range(4):
        offset = (rows * k) % 128
        start = rows * k - offset
        length = -(-(offset + rows) // 128) * 128
        for j, bd_ref in enumerate((first_ref, second_ref)):
            products[8 * group + 4 * j + k] = jnp.dot(bd_ref[:, start:start + length], shifted[k, :length, :],
                                                      preferred_element_type=jnp.float32)

    @pl.when(group == pl.num_programs(0) - 1)
    def _():
        core, at = where()
        own_ref[...] = jnp.zeros_like(own_ref)
        other_ref[...] = jnp.zeros_like(other_ref)
        column = lax.broadcasted_iota(jnp.int32, (count_d, 128), 1) // 16
        turned = [pltpu.roll(products[b], 16 * (b % 8), axis=1) if b % 8 else products[b] for b in range(16)]
        slabs = []
        for c in range(8):
            sides = []
            for side in (turned[:8], turned[8:]):
                picked = side[0]
                for b in range(1, 8):
                    picked = jnp.where(column == (c + b) % 8, side[b], picked)
                sides.append(pltpu.roll(picked, 128 - 16 * c, axis=1) if c else picked)
            slabs.append(jnp.concatenate(sides, axis=1))
        for which in range(CORES):
            @pl.when(core == which)
            def _():
                for c in range(8):
                    ref = own_ref if c // SIDE == which else other_ref
                    ref[(c - at["x"]) % SIDE, which * count_d:(which + 1) * count_d, :] = slabs[c]


def partial_integrals(bd, ac):
    rows = ac.shape[0]
    out = jax.ShapeDtypeStruct((SIDE, FRAME, 256), jnp.float32)
    whole = pl.BlockSpec(memory_space=pltpu.VMEM)
    return pl.pallas_call(
        partial_kernel,
        grid=(2,),
        out_shape=(out, out),
        in_specs=[pl.BlockSpec((bd.shape[0], 4 * rows), lambda g: (0, 2 * g)),
                  pl.BlockSpec((bd.shape[0], 4 * rows), lambda g: (0, 2 * g + 1)),
                  pl.BlockSpec(ac.shape, lambda g: (0, 0))],
        out_specs=(whole, whole),
        scratch_shapes=[pltpu.VMEM((4, -(-(rows + 96) // 128) * 128, 128), jnp.bfloat16),
                        pltpu.VMEM((16, bd.shape[0], 128), jnp.float32)],
        compiler_params=pltpu.CompilerParams(vmem_limit_bytes=48 * 2**20),
        cost_estimate=pl.CostEstimate(flops=10**9, bytes_accessed=8 * 10**6, transcendentals=0),
    )(bd, bd, ac)


def split(value):
    high = value.astype(jnp.bfloat16)
    return high, (value - high.astype(jnp.float32)).astype(jnp.bfloat16)


def arrange_kernel(amp_ref, high_ref, low_ref, amp, sems):
    step, steps = pl.program_id(0), pl.num_programs(0)
    slots, rows, _, width = amp.shape
    cut = rows // sems.shape[1]
    core, _ = where()

    def fetch(block):
        source = amp_ref.at[pl.ds(block * rows, rows), pl.ds(SIDE * core, SIDE)]
        slot = lax.rem(block, slots)
        return [pltpu.make_async_copy(source.at[pl.ds(k * cut, cut)], amp.at[slot, pl.ds(k * cut, cut)], sems.at[slot, k])
                for k in range(sems.shape[1])]

    @pl.when(step == 0)
    def _():
        for block in range(slots - 1):
            for copy in fetch(step + block):
                copy.start()

    @pl.when(step + slots - 1 < steps)
    def _():
        for copy in fetch(step + slots - 1):
            copy.start()

    for copy in fetch(step):
        copy.wait()
    pad = jnp.zeros((rows, WIDE - width), jnp.float32)
    for c in range(SIDE):
        high_ref[c], low_ref[c] = split(jnp.concatenate([amp[lax.rem(step, slots), :, c, :], pad], axis=1))


def arrange(amps, room):
    pairs, _, width = amps.shape
    rows, slots, cuts = 32, 3, 4
    out = jax.ShapeDtypeStruct((SIDE, pairs, WIDE), jnp.bfloat16)
    return pl.pallas_call(
        arrange_kernel,
        grid=(pairs // rows,),
        out_shape=(out, out),
        in_specs=[pl.BlockSpec(memory_space=pl.ANY)],
        out_specs=(pl.BlockSpec((SIDE, rows, WIDE), lambda i: (0, i, 0)),) * 2,
        scratch_shapes=[pltpu.VMEM((slots, rows, SIDE, width), jnp.float32), pltpu.SemaphoreType.DMA((slots, cuts))],
        compiler_params=pltpu.CompilerParams(vmem_limit_bytes=room * 2**20),
        cost_estimate=pl.CostEstimate(flops=10**6, bytes_accessed=15 * 10**6, transcendentals=0),
    )(amps)


def product(high, low, matrix):
    mhigh, mlow = split(matrix)
    dot = functools.partial(jnp.dot, preferred_element_type=jnp.float32)
    return dot(high, mhigh) + (dot(high, mlow) + dot(low, mhigh))


def slot(at, coord):
    ahead = (at - coord + SIDE) % SIDE
    return jnp.where(ahead == 0, 0, jnp.where(ahead == SIDE - 1, 1, ahead + 1))


def run_of(c, z, y):
    core, at = where()
    c, z, y = slot(c, at["x"]), slot(z, at["z"]), slot(y, at["y"])
    return jnp.where(core == 0, 16 * c + SIDE * z + y, 16 * z + SIDE * y + c)


def early_kernel(own_high, own_low, other_high, other_low, *refs):
    pieces, (out_ref, far_high, far_low, blocks, matrix, sems) = refs[:-6], refs[-6:]
    c = pl.program_id(0)

    @pl.when(c == 0)
    def _():
        copies, filled = [], 0
        for k, piece in enumerate(pieces):
            copies.append(pltpu.make_async_copy(piece, blocks.at[pl.ds(filled, piece.shape[0])], sems.at[k]))
            filled += piece.shape[0]
        for copy in copies:
            copy.start()
        out_ref[...] = jnp.zeros_like(out_ref)
        matrix[WIDE - 32:, :] = jnp.zeros((32, 256), jnp.float32)
        blocks[48:] = jnp.zeros((16,) + blocks.shape[1:], jnp.float32)
        for copy in copies:
            copy.wait()

    for z in range(SIDE):
        for y in range(SIDE):
            begin = CHIP_ROWS * (z * SIDE + y)
            matrix[begin:begin + FRAME, :] = blocks[run_of(c, z, y)]
    high = jnp.concatenate([own_high[...], other_high[...]], axis=0)
    low = jnp.concatenate([own_low[...], other_low[...]], axis=0)
    out_ref[...] += product(high, low, matrix[...])

    core, at = where()
    size = far_high.shape[1] // SIDE

    @pl.when(jnp.logical_and(core == 0, (at["x"] + 2) % SIDE == c))
    def _():
        for to, (one, two) in ((far_high, (own_high, other_high)), (far_low, (own_low, other_low))):
            to[:, :WIDE] = jnp.concatenate([one[...], two[...]], axis=0)
            to[:, WIDE:] = jnp.zeros((to.shape[0], SIDE * size - WIDE), jnp.bfloat16)

    @pl.when(core == 1)
    def _():
        start = jnp.minimum(SIDE * CHIP_ROWS * ((at["z"] + 2) % SIDE) // 128, (WIDE - size) // 128) * 128
        window = pl.ds(pl.multiple_of(start, 128), size)
        for to, (one, two) in ((far_high, (own_high, other_high)), (far_low, (own_low, other_low))):
            to[:, pl.ds(pl.multiple_of(size * c, 128), size)] = jnp.concatenate([one[:, window], two[:, window]], axis=0)


def early_ladder(own, other, pieces):
    pairs = own[0].shape[1]
    amp_spec = pl.BlockSpec((None, pairs, WIDE), lambda c: (c, 0, 0))
    far = jax.ShapeDtypeStruct((2 * pairs, SIDE * WINDOW), jnp.bfloat16)
    return pl.pallas_call(
        early_kernel,
        grid=(SIDE,),
        in_specs=[amp_spec] * 4 + [pl.BlockSpec(memory_space=pl.ANY)] * len(pieces),
        out_specs=(pl.BlockSpec(memory_space=pltpu.VMEM),) * 3,
        scratch_shapes=[pltpu.VMEM((64, FRAME, 256), jnp.float32), pltpu.VMEM((WIDE, 256), jnp.float32),
                        pltpu.SemaphoreType.DMA((len(pieces),))],
        out_shape=(jax.ShapeDtypeStruct((2 * pairs, 256), jnp.float32), far, far),
        compiler_params=pltpu.CompilerParams(vmem_limit_bytes=30 * 2**20),
        cost_estimate=pl.CostEstimate(flops=6 * 10**9, bytes_accessed=25 * 10**6, transcendentals=0),
    )(*own, *other, *pieces)


def late_kernel(high_ref, low_ref, up_ref, near_ref, far_ref, total_ref, own_ref, other_ref, matrix, far):
    pairs = total_ref.shape[0] // 2
    core, at = where()
    matrix[...] = jnp.zeros_like(matrix)
    far[:8] = up_ref[...]
    far[8:12] = near_ref[...]
    far[12:] = far_ref[...]

    @pl.when(core == 0)
    def _():
        for z in range(SIDE):
            for y in range(SIDE):
                begin = CHIP_ROWS * (z * SIDE + y)
                matrix[begin:begin + FRAME, :] = far[SIDE * slot(z, at["z"]) + slot(y, at["y"])]

    for z in range(SIDE):
        @pl.when(jnp.logical_and(core == 1, (at["z"] + 2) % SIDE == z))
        def _():
            first = SIDE * CHIP_ROWS * z
            offset = first - min(first // 128, (WIDE - WINDOW) // 128) * 128
            for c in range(SIDE):
                for y in range(SIDE):
                    to = WINDOW * c + offset + CHIP_ROWS * y
                    matrix[to:to + FRAME, :] = far[SIDE * slot(y, at["y"]) + slot(c, at["x"])]

    result = jnp.dot(total_ref[...] + product(high_ref[...], low_ref[...], matrix[...]),
                     reorder(256, 16).astype(jnp.float32), precision=lax.Precision.HIGHEST,
                     preferred_element_type=jnp.float32)
    own_ref[...] = result[:pairs]
    other_ref[...] = result[pairs:]


def late_ladder(high, low, pieces, total):
    out = jax.ShapeDtypeStruct((total.shape[0] // 2, 256), jnp.float32)
    whole = pl.BlockSpec(memory_space=pltpu.VMEM)
    return pl.pallas_call(
        late_kernel,
        in_specs=[whole] * (3 + len(pieces)),
        out_specs=(whole, whole),
        scratch_shapes=[pltpu.VMEM((SIDE * WINDOW, 256), jnp.float32), pltpu.VMEM((16, FRAME, 256), jnp.float32)],
        out_shape=(out, out),
        compiler_params=pltpu.CompilerParams(vmem_limit_bytes=32 * 2**20),
        cost_estimate=pl.CostEstimate(flops=2 * 10**9, bytes_accessed=8 * 10**6, transcendentals=0),
    )(high, low, *pieces, total)


def fetch(value, axes):
    far = permute(value, 2, axes)
    return [value, permute(value, 1, axes), permute(value, -1, axes), far]


def body(ac_factors, bd_factors, amplitudes):
    barrier = lax.optimization_barrier
    bd = bd_factors.reshape(bd_factors.shape[0], bd_factors.shape[2])
    mine, sent = partial_integrals(bd, ac_factors)
    chip = mine + permute(sent, 0, None)
    amplitudes, chip = barrier((amplitudes, chip))
    other = permute(amplitudes, 0, None)
    own = arrange(amplitudes, 44)
    shard = chip[0] + permute(chip[1], 1, "xx") + permute(chip[3], -1, "xx") + permute(chip[2], 2, "xx")

    shard, own = barrier((shard, own))
    line, other = barrier((fetch(shard, STEPS[0]), other))
    halves = [jnp.concatenate(part, axis=0) for part in (line[:2], line[2:])]
    up = [permute(half, 1, STEPS[1]) for half in halves]
    down = [permute(half, -1, STEPS[1]) for half in halves]
    far = [permute(up[0], 1, STEPS[1]), permute(down[1], -1, STEPS[1])]
    first, near = jnp.concatenate(halves + up, axis=0), jnp.concatenate(down, axis=0)
    up_first, down_near = permute(first, 1, STEPS[2]), permute(near, -1, STEPS[2])
    far, other = barrier((far, other))
    far = jnp.concatenate(far, axis=0)
    second = jnp.concatenate([near, far], axis=0)
    down_far = permute(far, -1, STEPS[2])
    up_second, down_first = permute(second, 1, STEPS[2]), permute(first, -1, STEPS[2])
    other = arrange(other, 16)
    up_first, other = barrier((up_first, other))
    far_up = permute(up_first, 1, STEPS[2])
    up_first, down_far = barrier((up_first, down_far))
    far_far = permute(down_far, -1, STEPS[2])
    down_near, down_first, up_second = barrier((down_near, down_first, up_second))
    far_down = [permute(down_near, -1, STEPS[2]), far_far]

    def runs(value):
        return value.reshape(-1, FRAME, 256)

    pieces = (first, second, up_first, up_second, down_first, down_near, down_far)
    total, high, low = early_ladder(own, other, [runs(v) for v in pieces])
    kept, given = late_ladder(high, low, [runs(v) for v in [far_up] + far_down], total)
    return kept + permute(given, 0, None)


def solution(mesh):
    placed = (P("aux", None), P("pair", "aux", None), P(("pair", "aux"), None, None))
    return jax.shard_map(
        body, mesh=mesh, in_specs=placed, out_specs=P(("pair", "aux"), None), check_vma=False
    )
```

```python
import functools

import jax
import jax.numpy as jnp
from jax import lax
from jax.experimental import pallas as pl
from jax.experimental.pallas import tpu as pltpu
from jax.sharding import PartitionSpec as P

AXES = ("pair", "aux")
SIDE = 4
CORES = 2
CHIP_ROWS = 150
FRAME = 152
STEPS = ("yx", "zy", "xz")
WINDOW = 768
WIDE = 2432


def place(z, y, core, x):
    return (((z % SIDE) * SIDE + y % SIDE) * CORES + core) * SIDE + x % SIDE


def permute(value, step, axes):
    pairs = []
    for z in range(SIDE):
        for y in range(SIDE):
            for core in range(CORES):
                for x in range(SIDE):
                    to = dict(z=z, y=y, core=core, x=x)
                    if step:
                        to[axes[core]] += step
                    else:
                        to["core"] = 1 - core
                    pairs.append((place(z, y, core, x), place(**to)))
    return lax.ppermute(value, AXES, pairs)


def where():
    pair = lax.axis_index("pair")
    return pair % CORES, dict(x=lax.axis_index("aux"), y=(pair // CORES) % SIDE, z=pair // (CORES * SIDE))


def reorder(size, across):
    row = lax.broadcasted_iota(jnp.int32, (size, size), 0)
    column = lax.broadcasted_iota(jnp.int32, (size, size), 1)
    return (row % across) * (size // across) + row // across == column


def partial_kernel(first_ref, second_ref, ac_ref, own_ref, other_ref, shifted, products):
    rows = ac_ref.shape[0]
    count_d = products.shape[1]
    group = pl.program_id(0)

    @pl.when(group == 0)
    def _():
        ordered = jnp.dot(ac_ref[...], reorder(128, 8).astype(jnp.bfloat16), preferred_element_type=jnp.float32)
        shifted[...] = jnp.zeros_like(shifted)
        for k in range(4):
            shifted[k, pl.ds((rows * k) % 128, rows), :] = ordered.astype(jnp.bfloat16)

    for k in range(4):
        offset = (rows * k) % 128
        start = rows * k - offset
        length = -(-(offset + rows) // 128) * 128
        for j, bd_ref in enumerate((first_ref, second_ref)):
            products[8 * group + 4 * j + k] = jnp.dot(bd_ref[:, start:start + length], shifted[k, :length, :],
                                                      preferred_element_type=jnp.float32)

    @pl.when(group == pl.num_programs(0) - 1)
    def _():
        core, at = where()
        own_ref[...] = jnp.zeros_like(own_ref)
        other_ref[...] = jnp.zeros_like(other_ref)
        column = lax.broadcasted_iota(jnp.int32, (count_d, 128), 1) // 16
        turned = [pltpu.roll(products[b], 16 * (b % 8), axis=1) if b % 8 else products[b] for b in range(16)]
        slabs = []
        for c in range(8):
            sides = []
            for side in (turned[:8], turned[8:]):
                picked = side[0]
                for b in range(1, 8):
                    picked = jnp.where(column == (c + b) % 8, side[b], picked)
                sides.append(pltpu.roll(picked, 128 - 16 * c, axis=1) if c else picked)
            slabs.append(jnp.concatenate(sides, axis=1))
        for which in range(CORES):
            @pl.when(core == which)
            def _():
                for c in range(8):
                    ref = own_ref if c // SIDE == which else other_ref
                    ref[(c - at["x"]) % SIDE, which * count_d:(which + 1) * count_d, :] = slabs[c]


def partial_integrals(bd, ac):
    rows = ac.shape[0]
    out = jax.ShapeDtypeStruct((SIDE, FRAME, 256), jnp.float32)
    whole = pl.BlockSpec(memory_space=pltpu.VMEM)
    return pl.pallas_call(
        partial_kernel,
        grid=(2,),
        out_shape=(out, out),
        in_specs=[pl.BlockSpec((bd.shape[0], 4 * rows), lambda g: (0, 2 * g)),
                  pl.BlockSpec((bd.shape[0], 4 * rows), lambda g: (0, 2 * g + 1)),
                  pl.BlockSpec(ac.shape, lambda g: (0, 0))],
        out_specs=(whole, whole),
        scratch_shapes=[pltpu.VMEM((4, -(-(rows + 96) // 128) * 128, 128), jnp.bfloat16),
                        pltpu.VMEM((16, bd.shape[0], 128), jnp.float32)],
        compiler_params=pltpu.CompilerParams(vmem_limit_bytes=48 * 2**20),
        cost_estimate=pl.CostEstimate(flops=10**9, bytes_accessed=8 * 10**6, transcendentals=0),
    )(bd, bd, ac)


def split(value):
    high = value.astype(jnp.bfloat16)
    return high, (value - high.astype(jnp.float32)).astype(jnp.bfloat16)


def arrange_kernel(amp_ref, high_ref, low_ref, amp, sems):
    step, steps = pl.program_id(0), pl.num_programs(0)
    slots, rows, _, width = amp.shape
    cut = rows // sems.shape[1]
    core, _ = where()

    def fetch(block):
        source = amp_ref.at[pl.ds(block * rows, rows), pl.ds(SIDE * core, SIDE)]
        slot = lax.rem(block, slots)
        return [pltpu.make_async_copy(source.at[pl.ds(k * cut, cut)], amp.at[slot, pl.ds(k * cut, cut)], sems.at[slot, k])
                for k in range(sems.shape[1])]

    @pl.when(step == 0)
    def _():
        for block in range(slots - 1):
            for copy in fetch(step + block):
                copy.start()

    @pl.when(step + slots - 1 < steps)
    def _():
        for copy in fetch(step + slots - 1):
            copy.start()

    for copy in fetch(step):
        copy.wait()
    pad = jnp.zeros((rows, WIDE - width), jnp.float32)
    for c in range(SIDE):
        high_ref[c], low_ref[c] = split(jnp.concatenate([amp[lax.rem(step, slots), :, c, :], pad], axis=1))


def arrange(amps, room):
    pairs, _, width = amps.shape
    rows, slots, cuts = 32, 3, 4
    out = jax.ShapeDtypeStruct((SIDE, pairs, WIDE), jnp.bfloat16)
    return pl.pallas_call(
        arrange_kernel,
        grid=(pairs // rows,),
        out_shape=(out, out),
        in_specs=[pl.BlockSpec(memory_space=pl.ANY)],
        out_specs=(pl.BlockSpec((SIDE, rows, WIDE), lambda i: (0, i, 0)),) * 2,
        scratch_shapes=[pltpu.VMEM((slots, rows, SIDE, width), jnp.float32), pltpu.SemaphoreType.DMA((slots, cuts))],
        compiler_params=pltpu.CompilerParams(vmem_limit_bytes=room * 2**20),
        cost_estimate=pl.CostEstimate(flops=10**6, bytes_accessed=15 * 10**6, transcendentals=0),
    )(amps)


def product(high, low, matrix):
    mhigh, mlow = split(matrix)
    dot = functools.partial(jnp.dot, preferred_element_type=jnp.float32)
    return dot(high, mhigh) + (dot(high, mlow) + dot(low, mhigh))


def slot(at, coord):
    ahead = (at - coord + SIDE) % SIDE
    return jnp.where(ahead == 0, 0, jnp.where(ahead == SIDE - 1, 1, ahead + 1))


def run_of(c, z, y):
    core, at = where()
    c, z, y = slot(c, at["x"]), slot(z, at["z"]), slot(y, at["y"])
    return jnp.where(core == 0, 16 * c + SIDE * z + y, 16 * z + SIDE * y + c)


def early_kernel(own_high, own_low, other_high, other_low, *refs):
    pieces, (out_ref, far_high, far_low, blocks, matrix, sems) = refs[:-6], refs[-6:]
    c = pl.program_id(0)

    @pl.when(c == 0)
    def _():
        copies, filled = [], 0
        for k, piece in enumerate(pieces):
            copies.append(pltpu.make_async_copy(piece, blocks.at[pl.ds(filled, piece.shape[0])], sems.at[k]))
            filled += piece.shape[0]
        for copy in copies:
            copy.start()
        out_ref[...] = jnp.zeros_like(out_ref)
        matrix[WIDE - 32:, :] = jnp.zeros((32, 256), jnp.float32)
        blocks[48:] = jnp.zeros((16,) + blocks.shape[1:], jnp.float32)
        for copy in copies:
            copy.wait()

    for z in range(SIDE):
        for y in range(SIDE):
            begin = CHIP_ROWS * (z * SIDE + y)
            matrix[begin:begin + FRAME, :] = blocks[run_of(c, z, y)]
    high = jnp.concatenate([own_high[...], other_high[...]], axis=0)
    low = jnp.concatenate([own_low[...], other_low[...]], axis=0)
    out_ref[...] += product(high, low, matrix[...])

    core, at = where()
    size = far_high.shape[1] // SIDE

    @pl.when(jnp.logical_and(core == 0, (at["x"] + 2) % SIDE == c))
    def _():
        for to, (one, two) in ((far_high, (own_high, other_high)), (far_low, (own_low, other_low))):
            to[:, :WIDE] = jnp.concatenate([one[...], two[...]], axis=0)
            to[:, WIDE:] = jnp.zeros((to.shape[0], SIDE * size - WIDE), jnp.bfloat16)

    @pl.when(core == 1)
    def _():
        start = jnp.minimum(SIDE * CHIP_ROWS * ((at["z"] + 2) % SIDE) // 128, (WIDE - size) // 128) * 128
        window = pl.ds(pl.multiple_of(start, 128), size)
        for to, (one, two) in ((far_high, (own_high, other_high)), (far_low, (own_low, other_low))):
            to[:, pl.ds(pl.multiple_of(size * c, 128), size)] = jnp.concatenate([one[:, window], two[:, window]], axis=0)


def early_ladder(own, other, pieces):
    pairs = own[0].shape[1]
    amp_spec = pl.BlockSpec((None, pairs, WIDE), lambda c: (c, 0, 0))
    far = jax.ShapeDtypeStruct((2 * pairs, SIDE * WINDOW), jnp.bfloat16)
    return pl.pallas_call(
        early_kernel,
        grid=(SIDE,),
        in_specs=[amp_spec] * 4 + [pl.BlockSpec(memory_space=pl.ANY)] * len(pieces),
        out_specs=(pl.BlockSpec(memory_space=pltpu.VMEM),) * 3,
        scratch_shapes=[pltpu.VMEM((64, FRAME, 256), jnp.float32), pltpu.VMEM((WIDE, 256), jnp.float32),
                        pltpu.SemaphoreType.DMA((len(pieces),))],
        out_shape=(jax.ShapeDtypeStruct((2 * pairs, 256), jnp.float32), far, far),
        compiler_params=pltpu.CompilerParams(vmem_limit_bytes=30 * 2**20),
        cost_estimate=pl.CostEstimate(flops=6 * 10**9, bytes_accessed=25 * 10**6, transcendentals=0),
    )(*own, *other, *pieces)


def late_kernel(high_ref, low_ref, up_ref, near_ref, far_ref, total_ref, own_ref, other_ref, matrix, far):
    pairs = total_ref.shape[0] // 2
    core, at = where()
    matrix[...] = jnp.zeros_like(matrix)
    far[:8] = up_ref[...]
    far[8:12] = near_ref[...]
    far[12:] = far_ref[...]

    @pl.when(core == 0)
    def _():
        for z in range(SIDE):
            for y in range(SIDE):
                begin = CHIP_ROWS * (z * SIDE + y)
                matrix[begin:begin + FRAME, :] = far[SIDE * slot(z, at["z"]) + slot(y, at["y"])]

    for z in range(SIDE):
        @pl.when(jnp.logical_and(core == 1, (at["z"] + 2) % SIDE == z))
        def _():
            first = SIDE * CHIP_ROWS * z
            offset = first - min(first // 128, (WIDE - WINDOW) // 128) * 128
            for c in range(SIDE):
                for y in range(SIDE):
                    to = WINDOW * c + offset + CHIP_ROWS * y
                    matrix[to:to + FRAME, :] = far[SIDE * slot(y, at["y"]) + slot(c, at["x"])]

    result = jnp.dot(total_ref[...] + product(high_ref[...], low_ref[...], matrix[...]),
                     reorder(256, 16).astype(jnp.float32), precision=lax.Precision.HIGHEST,
                     preferred_element_type=jnp.float32)
    own_ref[...] = result[:pairs]
    other_ref[...] = result[pairs:]


def late_ladder(high, low, pieces, total):
    out = jax.ShapeDtypeStruct((total.shape[0] // 2, 256), jnp.float32)
    whole = pl.BlockSpec(memory_space=pltpu.VMEM)
    return pl.pallas_call(
        late_kernel,
        in_specs=[whole] * (3 + len(pieces)),
        out_specs=(whole, whole),
        scratch_shapes=[pltpu.VMEM((SIDE * WINDOW, 256), jnp.float32), pltpu.VMEM((16, FRAME, 256), jnp.float32)],
        out_shape=(out, out),
        compiler_params=pltpu.CompilerParams(vmem_limit_bytes=32 * 2**20),
        cost_estimate=pl.CostEstimate(flops=2 * 10**9, bytes_accessed=8 * 10**6, transcendentals=0),
    )(high, low, *pieces, total)


def fetch(value, axes):
    far = permute(value, 2, axes)
    return [value, permute(value, 1, axes), permute(value, -1, axes), far]


def body(ac_factors, bd_factors, amplitudes):
    barrier = lax.optimization_barrier
    bd = bd_factors.reshape(bd_factors.shape[0], bd_factors.shape[2])
    mine, sent = partial_integrals(bd, ac_factors)
    chip = mine + permute(sent, 0, None)
    amplitudes, chip = barrier((amplitudes, chip))
    other = permute(amplitudes, 0, None)
    own = arrange(amplitudes, 44)
    shard = chip[0] + permute(chip[1], 1, "xx") + permute(chip[3], -1, "xx") + permute(chip[2], 2, "xx")

    shard, own = barrier((shard, own))
    line, other = barrier((fetch(shard, STEPS[0]), other))
    halves = [jnp.concatenate(part, axis=0) for part in (line[:2], line[2:])]
    up = [permute(half, 1, STEPS[1]) for half in halves]
    down = [permute(half, -1, STEPS[1]) for half in halves]
    far = [permute(up[0], 1, STEPS[1]), permute(down[1], -1, STEPS[1])]
    down, other = barrier((down, other))
    first, near = jnp.concatenate(halves + up, axis=0), jnp.concatenate(down, axis=0)
    up_first, down_near = permute(first, 1, STEPS[2]), permute(near, -1, STEPS[2])
    far = jnp.concatenate(far, axis=0)
    second = jnp.concatenate([near, far], axis=0)
    down_far = permute(far, -1, STEPS[2])
    up_second, down_first = permute(second, 1, STEPS[2]), permute(first, -1, STEPS[2])
    other = arrange(other, 16)
    up_first, other = barrier((up_first, other))
    far_up = permute(up_first, 1, STEPS[2])
    up_first, down_far = barrier((up_first, down_far))
    far_far = permute(down_far, -1, STEPS[2])
    down_near, down_first, up_second = barrier((down_near, down_first, up_second))
    far_down = [permute(down_near, -1, STEPS[2]), far_far]

    def runs(value):
        return value.reshape(-1, FRAME, 256)

    pieces = (first, second, up_first, up_second, down_first, down_near, down_far)
    total, high, low = early_ladder(own, other, [runs(v) for v in pieces])
    kept, given = late_ladder(high, low, [runs(v) for v in [far_up] + far_down], total)
    return kept + permute(given, 0, None)


def solution(mesh):
    placed = (P("aux", None), P("pair", "aux", None), P(("pair", "aux"), None, None))
    return jax.shard_map(
        body, mesh=mesh, in_specs=placed, out_specs=P(("pair", "aux"), None), check_vma=False
    )
```
